128 devices in a mesh: chan: 8 (over x, core), stn: 16 (over y, z).
Axes of the slice: x: 4, y: 4, z: 4, core: 2. Of those that a mesh axis runs over, the one named last changes fastest.
Arguments:
- voltages: bfloat16 [2, 1024, 535552], P(None, ('stn', 'chan')), may hold values from -6 to 6
- fir_taps: float32 [12, 1024], replicated, may hold values from -1.75 to 1.75
- band_start: int32 [8], replicated, may hold values from 0 to 1008, as said below
- band_count: int32 [8], replicated, may hold values from 1 to 16, as said below
- subarray: int32 [512], replicated, may hold values from 0 to 3
Outputs:
- visibilities: float32 [1024, 2, 128, 1024], P('stn', None, 'chan')
The draws below stay inside these ranges and needn't reach their ends.
Inputs may be any that keep to these rules, and one draw needn't show every extreme that they name: `band_start`: ranges of different groups may intersect; some group's range starts at channel 1024 - 16. `band_count`: one group has exactly 16 channels and another exactly 1.
All inputs are finite; a program needn't handle non-finite values.
Results may differ from the reference program's by a relative error of at most 0.0038.
Values may be sent and summed in bfloat16 or wider, within the bound.
A program may use at most 512 MiB of HBM per device.

```python
import math
import jax
import jax.numpy as jnp
from jax import lax

NST = 512
NIN = 1024
NFFT = 1024
TAPS = 12
SPECTRA = 512
CMAX = 16
NSUB = 4
GROUPS = 8
SAMPLES = 535552


def band_pair(key):
    keys = jax.random.split(jax.random.fold_in(key, 77), 5)
    starts = jax.random.randint(keys[0], (GROUPS,), 0, NFFT - CMAX + 1)
    counts = jax.random.randint(keys[1], (GROUPS,), 1, CMAX + 1)
    top_group = jax.random.randint(keys[2], (), 0, GROUPS)
    low_group = (top_group + jax.random.randint(keys[3], (), 1, GROUPS)) % GROUPS
    edge_group = jax.random.randint(keys[4], (), 0, GROUPS)
    indices = jnp.arange(GROUPS)
    counts = jnp.where(indices == top_group, CMAX, jnp.where(indices == low_group, 1, counts))
    starts = jnp.where(indices == edge_group, NFFT - CMAX, starts)
    return (starts.astype(jnp.int32), counts.astype(jnp.int32))


def draw_band_start(key, part):
    return band_pair(key)[0]


def draw_band_count(key, part):
    return band_pair(key)[1]


def with_ends(drawn, rng, least, largest):
    dims = drawn.shape
    spot = [jax.random.randint(jax.random.fold_in(rng, axis), (), 0, dims[axis]) for axis in range(len(dims))]
    drawn = drawn.at[tuple(spot)].set(least)
    longest = dims.index(max(dims))
    spot[longest] = (spot[longest] + 1) % dims[longest]
    return drawn.at[tuple(spot)].set(largest)


def levels(rng, extent, shards, smallest, top_value):
    factor_of, own = 1.0, jax.random.fold_in(rng, 6)
    for position, blocks in shards:
        heights = jnp.exp(jax.random.uniform(jax.random.fold_in(own, position), (blocks,), jnp.float32, smallest / len(shards), top_value / len(shards)))
        factor_of = factor_of * jnp.repeat(heights, extent[position] // blocks).reshape([-1 if axis == position else 1 for axis in range(len(extent))])
    return factor_of


def bell_draw(key, dims, spread, bound, cuts=(), kind=jnp.bfloat16):
    values = jax.random.normal(key, dims, jnp.float32) * spread
    if len(cuts) > 0:
        values = levels(key, dims, cuts, -0.22, 0.18) * values
    return jnp.clip(values, min=-bound, max=bound).astype(kind)


def setup_inputs(seed: int = 0) -> dict:
    key_of = jax.random.split(jax.random.key(seed), 6)
    voltages = bell_draw(key_of[0], (2, NIN, SAMPLES), 1.0, 6.0, ((1, 128),))
    fir_taps = bell_draw(key_of[1], (TAPS, NFFT), TAPS ** -0.5, 1.75, (), jnp.float32)
    band_start = draw_band_start(jax.random.fold_in(key_of[5], 71), 0)
    band_count = draw_band_count(jax.random.fold_in(key_of[5], 71), 0)
    subarray = with_ends(jax.random.randint(key_of[4], (NST,), 0, NSUB), jax.random.fold_in(key_of[4], 1), 0, NSUB - 1).astype(jnp.int32)
    return {"voltages": voltages, "fir_taps": fir_taps, "band_start": band_start, "band_count": band_count, "subarray": subarray}


def make_table(band_start, band_count):
    groups = band_start.shape[0]
    slot_ids = jnp.arange(groups * CMAX, dtype=jnp.int32)
    group_of = slot_ids // CMAX
    offset = slot_ids % CMAX
    onehot = (group_of[:, None] == jnp.arange(groups, dtype=jnp.int32)[None, :]).astype(jnp.int32)
    first_chan = lax.optimization_barrier(jnp.sum(onehot * band_start[None, :], axis=1))
    chan_count = lax.optimization_barrier(jnp.sum(onehot * band_count[None, :], axis=1))
    channel = first_chan + offset
    live_mask = (offset < chan_count).astype(jnp.float32)
    phase_int = jnp.arange(NFFT, dtype=jnp.int32)[None, :] * channel[:, None] % NFFT
    angles = phase_int.astype(jnp.float32) * jnp.float32(2.0 * math.pi / NFFT)
    scaling = live_mask[:, None] * jnp.float32(1.0 / math.sqrt(NFFT))
    cosine = jnp.cos(angles) * scaling
    sine_part = jnp.sin(angles) * scaling
    stacked = jnp.stack([jnp.stack([cosine, sine_part], axis=1), jnp.stack([-sine_part, cosine], axis=1)], axis=1)
    return stacked.astype(jnp.bfloat16)

def filter_frames(volt_block, fir_taps):
    width = volt_block.shape[1]
    framed = volt_block.reshape(2, width, SPECTRA + TAPS - 1, NFFT)

    def add_tap(tap_index, summed):
        window = lax.dynamic_slice_in_dim(framed, tap_index, SPECTRA, 2)
        weights = lax.dynamic_slice_in_dim(fir_taps, tap_index, 1, 0)
        return summed + window.astype(jnp.float32) * weights
    summed = lax.fori_loop(0, TAPS, add_tap, jnp.zeros((2, width, SPECTRA, NFFT), jnp.float32))
    return summed.astype(jnp.bfloat16)

def reference(voltages, fir_taps, band_start, band_count, subarray):
    dft_table = make_table(band_start, band_count)
    slots_all = dft_table.shape[0]
    block_size = 64
    block_count = NIN // block_size

    def channelize(block_index):
        volt_block = lax.dynamic_slice_in_dim(voltages, block_index * block_size, block_size, 1)
        frames = filter_frames(volt_block, fir_taps)
        spectra = lax.dot_general(dft_table.astype(jnp.float32), frames.astype(jnp.float32), (((2, 3), (0, 3)), ((), ())))
        return spectra.astype(jnp.bfloat16)
    blocks = lax.map(channelize, jnp.arange(block_count, dtype=jnp.int32))
    spectra = jnp.moveaxis(blocks, 0, 2).reshape(slots_all, 2, NIN, SPECTRA)

    def correlate(slot_spectra):
        values = slot_spectra.astype(jnp.float32)
        rotated = jnp.stack([values[1], -values[0]], axis=0)
        stacked = jnp.stack([values, rotated], axis=0)
        return jnp.einsum('orit,rjt->oij', stacked, values)
    correlated = lax.map(correlate, spectra)
    stations = jnp.repeat(subarray, 2)
    same_array = (stations[:, None] == stations[None, :]).astype(jnp.float32)
    correlations = jnp.transpose(correlated, (2, 1, 0, 3))
    return correlations * (same_array / SPECTRA)[:, None, None, :]
```

```python
import math

import jax
import jax.numpy as jnp
from jax import lax
from jax.experimental import pallas as pl
from jax.experimental.pallas import tpu as pltpu
from jax.sharding import PartitionSpec as P

NFFT = 1024
TAPS = 12
SPECTRA = 512
CMAX = 16
GROUPS = 8
STEP = 128
CHUNKS = SPECTRA // STEP
f32 = jnp.float32
bf16 = jnp.bfloat16
NT = (((1,), (1,)), ((), ()))


def fill_table(start_ref, count_ref, table):
    lane = lax.broadcasted_iota(jnp.int32, (8, 128), 1)
    channel = lane % CMAX
    scale = jnp.zeros((8, 128), f32)
    for g in range(GROUPS):
        here = lane // CMAX == g
        channel = jnp.where(here, channel + start_ref[g], channel)
        live = here & (lane % CMAX < count_ref[g])
        scale = jnp.where(live, f32(1.0 / math.sqrt(NFFT)), scale)
    row = lax.broadcasted_iota(jnp.int32, (8, 128), 0)

    def rows16(k, carry):
        cosines, sines = [], []
        for half in range(2):
            phase = ((row + (k * 16 + half * 8)) * channel) & (NFFT - 1)
            angle = phase.astype(f32) * f32(2.0 * math.pi / NFFT)
            cosines.append(jnp.cos(angle) * scale)
            sines.append(jnp.sin(angle) * scale)
        cosine = jnp.concatenate(cosines, 0).astype(bf16)
        sine = jnp.concatenate(sines, 0)
        top = pl.multiple_of(k * 16, 16)
        low = pl.multiple_of(NFFT + k * 16, 16)
        table[pl.ds(top, 16), 0:128] = cosine
        table[pl.ds(top, 16), 128:256] = (-sine).astype(bf16)
        table[pl.ds(low, 16), 0:128] = sine.astype(bf16)
        table[pl.ds(low, 16), 128:256] = cosine
        return carry

    lax.fori_loop(0, NFFT // 16, rows16, 0)


def filter_chunk(volt, taps8, frames, first):
    def strip(k, carry):
        part = k // 8
        column = (k % 8) * 128
        lanes = pl.ds(pl.multiple_of(column, 128), 128)
        taps = [taps8[p, :, lanes] for p in range(TAPS)]
        window = [
            volt[part, :, pl.ds(pl.multiple_of((first + j) * NFFT + column, 128), 128)].astype(f32)
            for j in range(STEP + TAPS - 1)
        ]
        pair = []
        for u in range(STEP):
            total = window[u] * taps[0]
            for p in range(1, TAPS):
                total = total + window[u + p] * taps[p]
            pair.append(total)
            if u % 2 == 1:
                frames[part, (u - 1) * 8 : (u + 1) * 8, lanes] = jnp.concatenate(pair, 0).astype(bf16)
                pair = []
        return carry

    lax.fori_loop(0, 16, strip, 0)


def channelize_kernel(start_ref, count_ref, taps_ref, volt_hbm, out_ref, volt, taps8, table, frames, mixed, sorted_, sem):
    copies = []
    for c in range(CHUNKS):
        low = 0 if c == 0 else (c * STEP + TAPS - 1) * NFFT
        high = ((c + 1) * STEP + TAPS - 1) * NFFT
        copy = pltpu.make_async_copy(volt_hbm.at[:, :, low:high], volt.at[:, :, low:high], sem.at[c])
        copy.start()
        copies.append(copy)
    for p in range(TAPS):
        taps8[p] = jnp.broadcast_to(taps_ref[p : p + 1, :], (8, NFFT))
    fill_table(start_ref, count_ref, table)
    for c in range(CHUNKS):
        copies[c].wait()
        filter_chunk(volt, taps8, frames, c * STEP)
        product = jnp.dot(frames[0], table[0:NFFT, :], preferred_element_type=f32)
        product = product + jnp.dot(frames[1], table[NFFT:, :], preferred_element_type=f32)
        for o in range(2):
            mixed[o] = product[:, o * 128 : (o + 1) * 128]
            for i in range(8):
                sorted_[o, pl.ds(i, 128, stride=8), :] = mixed[o, pl.ds(i, STEP, stride=8), :].T
            tile = sorted_[o].reshape(GROUPS, CMAX, 8, STEP).astype(bf16)
            out_ref[:, c, :, :, o * 128 : (o + 1) * 128] = tile


def channelize(voltages, fir_taps, band_start, band_count):
    return pl.pallas_call(
        channelize_kernel,
        name="channelize",
        out_shape=jax.ShapeDtypeStruct((GROUPS, CHUNKS, CMAX, 8, 2 * STEP), bf16),
        in_specs=[pl.BlockSpec(memory_space=pltpu.SMEM)] * 2
        + [pl.BlockSpec(memory_space=pltpu.VMEM), pl.BlockSpec(memory_space=pl.ANY)],
        out_specs=pl.BlockSpec(memory_space=pltpu.VMEM),
        scratch_shapes=[
            pltpu.VMEM(voltages.shape, bf16),
            pltpu.VMEM((TAPS, 8, NFFT), f32),
            pltpu.VMEM((2 * NFFT, 256), bf16),
            pltpu.VMEM((2, STEP * 8, NFFT), bf16),
            pltpu.VMEM((2, STEP * 8, 128), f32),
            pltpu.VMEM((2, 128 * 8, 128), f32),
            pltpu.SemaphoreType.DMA((CHUNKS,)),
        ],
        compiler_params=pltpu.CompilerParams(vmem_limit_bytes=58 << 20),
    )(band_start, band_count, fir_taps, voltages)


def correlate_kernel(row_ref, all_ref, out_ref):
    total = None
    for c in range(CHUNKS):
        rows = row_ref[c]
        turned = jnp.concatenate([rows[:, STEP:], -rows[:, :STEP]], axis=1)
        both = jnp.concatenate([rows, turned], axis=0)
        part = lax.dot_general(both, all_ref[c], NT, preferred_element_type=f32)
        total = part if total is None else total + part
    out_ref[0] = total.reshape(2, row_ref.shape[1], -1).astype(bf16)


def correlate(spectra, blocks):
    inputs = spectra.shape[1]
    rows = inputs // blocks
    return pl.pallas_call(
        correlate_kernel,
        name="correlate",
        grid=(blocks,),
        out_shape=jax.ShapeDtypeStruct((blocks, 2, rows, inputs), bf16),
        in_specs=[
            pl.BlockSpec((CHUNKS, rows, 2 * STEP), lambda k: (0, k, 0)),
            pl.BlockSpec(memory_space=pltpu.VMEM),
        ],
        out_specs=pl.BlockSpec((1, 2, rows, inputs), lambda k: (k, 0, 0, 0)),
        compiler_params=pltpu.CompilerParams(vmem_limit_bytes=40 << 20),
    )(spectra, spectra)


def place_kernel(in_ref, mask_ref, out_ref, scratch):
    mask = mask_ref[...]
    for q in range(CMAX):
        for o in range(2):
            values = in_ref[q, o].astype(f32) * mask
            for part in range(8):
                for half in range(2):
                    scratch[part, pl.ds(half * 256 + o * 16 + q, 8, stride=32), :] = values[
                        half * 8 : (half + 1) * 8, part * 128 : (part + 1) * 128
                    ]
    for part in range(8):
        out_ref[:, part * 128 : (part + 1) * 128] = scratch[part]


def place(blocks, mask):
    slots, _, rows, inputs = blocks.shape
    flat = pl.pallas_call(
        place_kernel,
        name="place",
        grid=(rows // 16,),
        out_shape=jax.ShapeDtypeStruct((rows * 2 * slots, inputs), f32),
        in_specs=[
            pl.BlockSpec((slots, 2, 16, inputs), lambda b: (0, 0, b, 0)),
            pl.BlockSpec((16, inputs), lambda b: (b, 0)),
        ],
        out_specs=pl.BlockSpec((16 * 2 * slots, inputs), lambda b: (b, 0)),
        scratch_shapes=[pltpu.VMEM((8, 16 * 2 * slots, 128), f32)],
        compiler_params=pltpu.CompilerParams(vmem_limit_bytes=40 << 20),
    )(blocks, mask)
    return flat.reshape(rows, 2, slots, inputs)


def per_device(voltages, fir_taps, band_start, band_count, subarray):
    spectra = channelize(voltages, fir_taps, band_start, band_count)
    spectra = lax.all_to_all(spectra, "chan", split_axis=0, concat_axis=0, tiled=True)
    spectra = jnp.transpose(spectra, (2, 1, 0, 3, 4))
    spectra = lax.all_to_all(spectra, "stn", split_axis=0, concat_axis=0, tiled=True)
    spectra = jnp.transpose(spectra, (1, 0, 2, 3, 4)).reshape(CHUNKS, -1, 2 * STEP)
    blocks = correlate(spectra, lax.axis_size("stn"))
    blocks = lax.all_to_all(blocks, "stn", split_axis=0, concat_axis=0, tiled=True)
    rows = blocks.shape[2]
    stations = jnp.repeat(subarray, 2)
    own = lax.dynamic_slice_in_dim(stations, lax.axis_index("stn") * rows, rows, 0)
    mask = (own[:, None] == stations[None, :]).astype(f32) / SPECTRA
    return place(blocks, mask)


def solution(mesh):
    in_specs = (P(None, ("stn", "chan"), None), P(), P(), P(), P())
    out_specs = P("stn", None, "chan", None)
    return jax.shard_map(
        per_device, mesh=mesh, in_specs=in_specs, out_specs=out_specs, check_vma=False
    )
```

```python
import math

import jax
import jax.numpy as jnp
from jax import lax
from jax.experimental import pallas as pl
from jax.experimental.pallas import tpu as pltpu
from jax.sharding import PartitionSpec as P

NFFT = 1024
TAPS = 12
SPECTRA = 512
CMAX = 16
GROUPS = 8
STEP = 128
CHUNKS = SPECTRA // STEP
f32 = jnp.float32
bf16 = jnp.bfloat16
MESH = pl.DeviceIdType.MESH
NT = (((1,), (1,)), ((), ()))


def fill_table(start_ref, count_ref, table):
    lane = lax.broadcasted_iota(jnp.int32, (8, 128), 1)
    channel = lane % CMAX
    scale = jnp.zeros((8, 128), f32)
    for g in range(GROUPS):
        here = lane // CMAX == g
        channel = jnp.where(here, channel + start_ref[g], channel)
        live = here & (lane % CMAX < count_ref[g])
        scale = jnp.where(live, f32(1.0 / math.sqrt(NFFT)), scale)
    row = lax.broadcasted_iota(jnp.int32, (8, 128), 0)

    def rows16(k, carry):
        cosines, sines = [], []
        for half in range(2):
            phase = ((row + (k * 16 + half * 8)) * channel) & (NFFT - 1)
            angle = phase.astype(f32) * f32(2.0 * math.pi / NFFT)
            cosines.append(jnp.cos(angle) * scale)
            sines.append(jnp.sin(angle) * scale)
        cosine = jnp.concatenate(cosines, 0).astype(bf16)
        sine = jnp.concatenate(sines, 0)
        top = pl.multiple_of(k * 16, 16)
        low = pl.multiple_of(NFFT + k * 16, 16)
        table[pl.ds(top, 16), 0:128] = cosine
        table[pl.ds(top, 16), 128:256] = (-sine).astype(bf16)
        table[pl.ds(low, 16), 0:128] = sine.astype(bf16)
        table[pl.ds(low, 16), 128:256] = cosine
        return carry

    lax.fori_loop(0, NFFT // 16, rows16, 0)


def filter_chunk(volt, taps8, frames, first):
    def strip(k, carry):
        part = k // 8
        column = (k % 8) * 128
        lanes = pl.ds(pl.multiple_of(column, 128), 128)
        taps = [taps8[p, :, lanes] for p in range(TAPS)]
        window = [
            volt[part, :, pl.ds(pl.multiple_of((first + j) * NFFT + column, 128), 128)].astype(f32)
            for j in range(STEP + TAPS - 1)
        ]
        pair = []
        for u in range(STEP):
            total = window[u] * taps[0]
            for p in range(1, TAPS):
                total = total + window[u + p] * taps[p]
            pair.append(total)
            if u % 2 == 1:
                frames[part, (u - 1) * 8 : (u + 1) * 8, lanes] = jnp.concatenate(pair, 0).astype(bf16)
                pair = []
        return carry

    lax.fori_loop(0, 16, strip, 0)


def total_wait(ref, sem):
    pltpu.make_async_copy(ref, ref, sem).wait()


def correlator_kernel(
    start_ref, count_ref, taps_ref, volt_hbm, out_ref,
    volt, taps8, table, frames, mixed, sorted_, outgoing, passing, held, results,
    volt_sem, send_a, recv_a, send_b, recv_b, send_c, recv_c,
):
    chan, stn = lax.axis_index("chan"), lax.axis_index("stn")
    chans, stns = lax.axis_size("chan"), lax.axis_size("stn")

    def volt_copy(c, first):
        low = first * NFFT
        wide = STEP * NFFT
        span = pl.ds(pl.multiple_of(low, 128), wide)
        return pltpu.make_async_copy(volt_hbm.at[:, :, span], volt.at[:, :, span], volt_sem.at[c])

    halo = pl.ds(SPECTRA * NFFT, (TAPS - 1) * NFFT)
    halo_copy = pltpu.make_async_copy(volt_hbm.at[:, :, halo], volt.at[:, :, halo], volt_sem.at[CHUNKS])
    for c in range(CHUNKS):
        volt_copy(c, c * STEP).start()
    halo_copy.start()

    barrier = pltpu.get_barrier_semaphore()
    for d in range(1, chans):
        pl.semaphore_signal(barrier, inc=1, device_id=((chan + d) % chans, stn), device_id_type=MESH)
    for d in range(1, stns):
        pl.semaphore_signal(barrier, inc=1, device_id=(chan, (stn + d) % stns), device_id_type=MESH)

    for p in range(TAPS):
        taps8[p] = jnp.broadcast_to(taps_ref[p : p + 1, :], (8, NFFT))
    fill_table(start_ref, count_ref, table)
    pl.semaphore_wait(barrier, chans + stns - 2)

    def send_chan(c):
        for d in range(1, chans):
            to = (chan + d) % chans
            pltpu.make_async_remote_copy(
                outgoing.at[c, to], passing.at[c, chan], send_a, recv_a.at[c],
                device_id=(to, stn), device_id_type=MESH,
            ).start()
        pltpu.make_async_copy(outgoing.at[c, chan], passing.at[c, chan], recv_a.at[c]).start()

    def send_stn(c):
        total_wait(passing.at[c], recv_a.at[c])
        for d in range(1, stns):
            to = (stn + d) % stns
            pltpu.make_async_remote_copy(
                passing.at[c, :, to], held.at[c, stn], send_b, recv_b.at[c],
                device_id=(chan, to), device_id_type=MESH,
            ).start()
        pltpu.make_async_copy(passing.at[c, :, stn], held.at[c, stn], recv_b.at[c]).start()

    volt_copy(0, 0).wait()

    def chunk(c, carry):
        @pl.when(c < CHUNKS - 1)
        def _():
            volt_copy(c + 1, (c + 1) * STEP).wait()

        @pl.when(c == CHUNKS - 1)
        def _():
            halo_copy.wait()

        filter_chunk(volt, taps8, frames, c * STEP)
        product = jnp.dot(frames[0], table[0:NFFT, :], preferred_element_type=f32)
        product = product + jnp.dot(frames[1], table[NFFT:, :], preferred_element_type=f32)
        for o in range(2):
            mixed[o] = product[:, o * 128 : (o + 1) * 128]
            for i in range(8):
                sorted_[o, pl.ds(i, 128, stride=8), :] = mixed[o, pl.ds(i, STEP, stride=8), :].T
            tile = sorted_[o].reshape(GROUPS, CMAX, 8, STEP).astype(bf16)
            outgoing[c, :, :, :, o * 128 : (o + 1) * 128] = tile
        send_chan(c)

        @pl.when(c > 0)
        def _():
            send_stn(c - 1)

        return carry

    lax.fori_loop(0, CHUNKS, chunk, 0)
    send_stn(CHUNKS - 1)
    for c in range(CHUNKS):
        total_wait(held.at[c], recv_b.at[c])

    inputs = stns * chans * 8
    rows = chans * 8

    def correlate(s, carry):
        k = (stn + 7 * (s + 1)) % stns
        total = None
        for c in range(CHUNKS):
            own = held[c, k].reshape(rows, 2 * STEP)
            turned = jnp.concatenate([own[:, STEP:], -own[:, :STEP]], axis=1)
            both = jnp.concatenate([own, turned], axis=0)
            part = lax.dot_general(
                both, held[c].reshape(inputs, 2 * STEP), NT, preferred_element_type=f32
            )
            total = part if total is None else total + part
        results[k] = total.reshape(2, rows, inputs).astype(bf16)

        @pl.when(s < stns - 1)
        def _():
            pltpu.make_async_remote_copy(
                results.at[k], out_ref.at[stn], send_c, recv_c,
                device_id=(chan, k), device_id_type=MESH,
            ).start()

        @pl.when(s == stns - 1)
        def _():
            pltpu.make_async_copy(results.at[k], out_ref.at[stn], recv_c).start()

        return carry

    lax.fori_loop(0, stns, correlate, 0)
    total_wait(outgoing.at[:, 0 : chans - 1], send_a)
    total_wait(held.at[:, 0 : stns - 1], send_b)
    total_wait(results.at[0 : stns - 1], send_c)
    total_wait(out_ref, recv_c)


def correlator(voltages, fir_taps, band_start, band_count):
    chans, stns = lax.axis_size("chan"), lax.axis_size("stn")
    inputs = stns * chans * 8
    blocks = (stns, 2, chans * 8, inputs)
    return pl.pallas_call(
        correlator_kernel,
        name="correlator",
        out_shape=jax.ShapeDtypeStruct(blocks, bf16),
        in_specs=[pl.BlockSpec(memory_space=pltpu.SMEM)] * 2
        + [pl.BlockSpec(memory_space=pltpu.VMEM), pl.BlockSpec(memory_space=pl.ANY)],
        out_specs=pl.BlockSpec(memory_space=pl.ANY),
        scratch_shapes=[
            pltpu.VMEM(voltages.shape, bf16),
            pltpu.VMEM((TAPS, 8, NFFT), f32),
            pltpu.VMEM((2 * NFFT, 256), bf16),
            pltpu.VMEM((2, STEP * 8, NFFT), bf16),
            pltpu.VMEM((2, STEP * 8, 128), f32),
            pltpu.VMEM((2, 128 * 8, 128), f32),
            pltpu.VMEM((CHUNKS, chans, CMAX, 8, 2 * STEP), bf16),
            pltpu.VMEM((CHUNKS, chans, CMAX, 8, 2 * STEP), bf16),
            pltpu.VMEM((CHUNKS, stns, chans, 8, 2 * STEP), bf16),
            pltpu.VMEM(blocks, bf16),
            pltpu.SemaphoreType.DMA((CHUNKS + 1,)),
            pltpu.SemaphoreType.DMA,
            pltpu.SemaphoreType.DMA((CHUNKS,)),
            pltpu.SemaphoreType.DMA,
            pltpu.SemaphoreType.DMA((CHUNKS,)),
            pltpu.SemaphoreType.DMA,
            pltpu.SemaphoreType.DMA,
        ],
        compiler_params=pltpu.CompilerParams(
            collective_id=0, has_side_effects=True, vmem_limit_bytes=58 << 20
        ),
    )(band_start, band_count, fir_taps, voltages)


def place_kernel(in_ref, mask_ref, out_ref, scratch):
    mask = mask_ref[...]
    for q in range(CMAX):
        for o in range(2):
            values = in_ref[q, o].astype(f32) * mask
            for part in range(8):
                for half in range(2):
                    scratch[part, pl.ds(half * 256 + o * 16 + q, 8, stride=32), :] = values[
                        half * 8 : (half + 1) * 8, part * 128 : (part + 1) * 128
                    ]
    for part in range(8):
        out_ref[:, part * 128 : (part + 1) * 128] = scratch[part]


def place(blocks, mask):
    slots, _, rows, inputs = blocks.shape
    flat = pl.pallas_call(
        place_kernel,
        name="place",
        grid=(rows // 16,),
        out_shape=jax.ShapeDtypeStruct((rows * 2 * slots, inputs), f32),
        in_specs=[
            pl.BlockSpec((slots, 2, 16, inputs), lambda b: (0, 0, b, 0)),
            pl.BlockSpec((16, inputs), lambda b: (b, 0)),
        ],
        out_specs=pl.BlockSpec((16 * 2 * slots, inputs), lambda b: (b, 0)),
        scratch_shapes=[pltpu.VMEM((8, 16 * 2 * slots, 128), f32)],
        compiler_params=pltpu.CompilerParams(vmem_limit_bytes=40 << 20),
    )(blocks, mask)
    return flat.reshape(rows, 2, slots, inputs)


def per_device(voltages, fir_taps, band_start, band_count, subarray):
    blocks = correlator(voltages, fir_taps, band_start, band_count)
    rows = blocks.shape[2]
    stations = jnp.repeat(subarray, 2)
    own = lax.dynamic_slice_in_dim(stations, lax.axis_index("stn") * rows, rows, 0)
    mask = (own[:, None] == stations[None, :]).astype(f32) / SPECTRA
    return place(blocks, mask)


def solution(mesh):
    in_specs = (P(None, ("stn", "chan"), None), P(), P(), P(), P())
    out_specs = P("stn", None, "chan", None)
    return jax.shard_map(
        per_device, mesh=mesh, in_specs=in_specs, out_specs=out_specs, check_vma=False
    )
```

```python
import functools
import math

import jax
import jax.numpy as jnp
from jax import lax
from jax.experimental import pallas as pl
from jax.experimental.pallas import tpu as pltpu
from jax.sharding import PartitionSpec as P

NFFT = 1024
TAPS = 12
SPECTRA = 512
CMAX = 16
GROUPS = 8
STEP = 128
CHUNKS = SPECTRA // STEP
ROOM = 384
NSUB = 4
f32 = jnp.float32
bf16 = jnp.bfloat16
MESH = pl.DeviceIdType.MESH
NT = (((1,), (1,)), ((), ()))


def fill_table(start_ref, count_ref, table):
    lane = lax.broadcasted_iota(jnp.int32, (8, 128), 1)
    channel = lane % CMAX
    scale = jnp.zeros((8, 128), f32)
    for g in range(GROUPS):
        here = lane // CMAX == g
        channel = jnp.where(here, channel + start_ref[g], channel)
        live = here & (lane % CMAX < count_ref[g])
        scale = jnp.where(live, f32(1.0 / math.sqrt(NFFT)), scale)
    row = lax.broadcasted_iota(jnp.int32, (8, 128), 0)

    def rows16(k, carry):
        cosines, sines = [], []
        for half in range(2):
            phase = ((row + (k * 16 + half * 8)) * channel) & (NFFT - 1)
            angle = phase.astype(f32) * f32(2.0 * math.pi / NFFT)
            cosines.append(jnp.cos(angle) * scale)
            sines.append(jnp.sin(angle) * scale)
        cosine = jnp.concatenate(cosines, 0).astype(bf16)
        sine = jnp.concatenate(sines, 0)
        top = pl.multiple_of(k * 16, 16)
        low = pl.multiple_of(NFFT + k * 16, 16)
        table[pl.ds(top, 16), 0:128] = cosine
        table[pl.ds(top, 16), 128:256] = (-sine).astype(bf16)
        table[pl.ds(low, 16), 0:128] = sine.astype(bf16)
        table[pl.ds(low, 16), 128:256] = cosine
        return carry

    lax.fori_loop(0, NFFT // 16, rows16, 0)


def filter_chunk(volt, taps8, frames, first):
    def strip(k, carry):
        part = k // 8
        column = (k % 8) * 128
        lanes = pl.ds(pl.multiple_of(column, 128), 128)
        taps = [taps8[p, :, lanes] for p in range(TAPS)]
        window = [
            volt[part, :, pl.ds(pl.multiple_of((first + j) * NFFT + column, 128), 128)].astype(f32)
            for j in range(STEP + TAPS - 1)
        ]
        pair = []
        for u in range(STEP):
            total = window[u] * taps[0]
            for p in range(1, TAPS):
                total = total + window[u + p] * taps[p]
            pair.append(total)
            if u % 2 == 1:
                frames[part, (u - 1) * 8 : (u + 1) * 8, lanes] = jnp.concatenate(pair, 0).astype(bf16)
                pair = []
        return carry

    lax.fori_loop(0, 16, strip, 0)


def fill_picker(target_ref, picker):
    target = target_ref[...]

    def rows16(k, carry):
        top = pl.multiple_of(k * 16, 16)
        row = lax.broadcasted_iota(jnp.int32, (16, target.shape[1]), 0) + top
        picker[pl.ds(top, 16), :] = jnp.where(row == target, f32(1), f32(0)).astype(bf16)
        return carry

    lax.fori_loop(0, NSUB * ROOM // 16, rows16, 0)


def total_wait(ref, sem):
    pltpu.make_async_copy(ref, ref, sem).wait()


def correlator_kernel(
    packed, start_ref, count_ref, taps_ref, target_ref, member_ref, volt_hbm, out_ref,
    volt, taps8, table, frames, mixed, sorted_, outgoing, passing, held, results,
    picker, picked, summed, volt_sem, send_a, recv_a, send_b, recv_b, send_c, recv_c,
):
    chan, stn = lax.axis_index("chan"), lax.axis_index("stn")
    chans, stns = lax.axis_size("chan"), lax.axis_size("stn")

    def volt_copy(c, first):
        low = first * NFFT
        wide = STEP * NFFT
        span = pl.ds(pl.multiple_of(low, 128), wide)
        return pltpu.make_async_copy(volt_hbm.at[:, :, span], volt.at[:, :, span], volt_sem.at[c])

    halo = pl.ds(SPECTRA * NFFT, (TAPS - 1) * NFFT)
    halo_copy = pltpu.make_async_copy(volt_hbm.at[:, :, halo], volt.at[:, :, halo], volt_sem.at[CHUNKS])
    for c in range(CHUNKS):
        volt_copy(c, c * STEP).start()
    halo_copy.start()

    barrier = pltpu.get_barrier_semaphore()
    for d in range(1, chans):
        pl.semaphore_signal(barrier, inc=1, device_id=((chan + d) % chans, stn), device_id_type=MESH)
    for d in range(1, stns):
        pl.semaphore_signal(barrier, inc=1, device_id=(chan, (stn + d) % stns), device_id_type=MESH)

    for p in range(TAPS):
        taps8[p] = jnp.broadcast_to(taps_ref[p : p + 1, :], (8, NFFT))
    fill_table(start_ref, count_ref, table)
    if packed:
        fill_picker(target_ref, picker)
    pl.semaphore_wait(barrier, chans + stns - 2)

    def send_chan(c):
        for d in range(1, chans):
            to = (chan + d) % chans
            pltpu.make_async_remote_copy(
                outgoing.at[c, to], passing.at[c, chan], send_a, recv_a.at[c],
                device_id=(to, stn), device_id_type=MESH,
            ).start()
        pltpu.make_async_copy(outgoing.at[c, chan], passing.at[c, chan], recv_a.at[c]).start()

    def send_stn(c):
        total_wait(passing.at[c], recv_a.at[c])
        for d in range(1, stns):
            to = (stn + d) % stns
            pltpu.make_async_remote_copy(
                passing.at[c, :, to], held.at[c, stn], send_b, recv_b.at[c],
                device_id=(chan, to), device_id_type=MESH,
            ).start()
        pltpu.make_async_copy(passing.at[c, :, stn], held.at[c, stn], recv_b.at[c]).start()

    volt_copy(0, 0).wait()

    def chunk(c, carry):
        @pl.when(c < CHUNKS - 1)
        def _():
            volt_copy(c + 1, (c + 1) * STEP).wait()

        @pl.when(c == CHUNKS - 1)
        def _():
            halo_copy.wait()

        filter_chunk(volt, taps8, frames, c * STEP)
        product = jnp.dot(frames[0], table[0:NFFT, :], preferred_element_type=f32)
        product = product + jnp.dot(frames[1], table[NFFT:, :], preferred_element_type=f32)
        for o in range(2):
            mixed[o] = product[:, o * 128 : (o + 1) * 128]
            for i in range(8):
                sorted_[o, pl.ds(i, 128, stride=8), :] = mixed[o, pl.ds(i, STEP, stride=8), :].T
            tile = sorted_[o].reshape(GROUPS, CMAX, 8, STEP).astype(bf16)
            outgoing[c, :, :, :, o * 128 : (o + 1) * 128] = tile
        send_chan(c)

        @pl.when(c > 0)
        def _():
            send_stn(c - 1)

        return carry

    lax.fori_loop(0, CHUNKS, chunk, 0)
    inputs = stns * chans * 8
    rows = chans * 8
    quad = 4

    def pick(c):
        total_wait(held.at[c], recv_b.at[c])
        everyone = held[c].reshape(inputs, 2 * STEP)
        picked[c] = jnp.dot(picker[...], everyone, preferred_element_type=f32).astype(bf16)

    def add_up(c, b):
        own = held[c, pl.ds(b * quad, quad)].reshape(quad * rows, 2 * STEP)
        turned = jnp.concatenate([own[:, STEP:], -own[:, :STEP]], axis=1)
        for o, left in enumerate((own, turned)):
            wide = lax.dot_general(left, picked[c], NT, preferred_element_type=f32)
            member = member_ref[pl.ds(pl.multiple_of(b * quad * rows, 8), quad * rows), :]
            chosen = wide[:, 0:ROOM]
            for n in range(1, NSUB):
                chosen = jnp.where(member == n, wide[:, n * ROOM : (n + 1) * ROOM], chosen)
            chosen = chosen.reshape(quad, rows, ROOM)
            if c > 0:
                chosen = chosen + summed[pl.ds(b * quad, quad), o]
            if c < CHUNKS - 1:
                summed[pl.ds(b * quad, quad), o] = chosen
            else:
                results[pl.ds(b * quad, quad), o] = chosen.astype(bf16)

    def return_rows(k):
        @pl.when(k != stn)
        def _():
            pltpu.make_async_remote_copy(
                results.at[k], out_ref.at[stn], send_c, recv_c,
                device_id=(chan, k), device_id_type=MESH,
            ).start()

        @pl.when(k == stn)
        def _():
            pltpu.make_async_copy(results.at[k], out_ref.at[stn], recv_c).start()

    if packed:
        send_stn(CHUNKS - 1)
        for c in range(CHUNKS):
            pick(c)

            def add_block(s, carry, c=c):
                b = (stn // quad + 1 + s) % (stns // quad)
                add_up(c, b)
                if c == CHUNKS - 1:
                    for e in range(quad):
                        return_rows(b * quad + e)
                return carry

            lax.fori_loop(0, stns // quad, add_block, 0)
    else:
        send_stn(CHUNKS - 1)
        for c in range(CHUNKS):
            total_wait(held.at[c], recv_b.at[c])

    def correlate(s, carry):
        k = (stn + 7 * (s + 1)) % stns
        total = None
        for c in range(CHUNKS):
            own = held[c, k].reshape(rows, 2 * STEP)
            turned = jnp.concatenate([own[:, STEP:], -own[:, :STEP]], axis=1)
            both = jnp.concatenate([own, turned], axis=0)
            part = lax.dot_general(
                both, held[c].reshape(inputs, 2 * STEP), NT, preferred_element_type=f32
            )
            total = part if total is None else total + part
        results[k] = total.reshape(2, rows, inputs).astype(bf16)

        return_rows(k)
        return carry

    if not packed:
        lax.fori_loop(0, stns, correlate, 0)
    total_wait(outgoing.at[:, 0 : chans - 1], send_a)
    total_wait(held.at[:, 0 : stns - 1], send_b)
    total_wait(results.at[0 : stns - 1], send_c)
    total_wait(out_ref, recv_c)


def correlator(packed, voltages, fir_taps, band_start, band_count, target, member):
    chans, stns = lax.axis_size("chan"), lax.axis_size("stn")
    inputs = stns * chans * 8
    blocks = (stns, 2, chans * 8, ROOM if packed else inputs)
    return pl.pallas_call(
        functools.partial(correlator_kernel, packed),
        name="correlator_packed" if packed else "correlator",
        out_shape=jax.ShapeDtypeStruct(blocks, bf16),
        in_specs=[pl.BlockSpec(memory_space=pltpu.SMEM)] * 2
        + [pl.BlockSpec(memory_space=pltpu.VMEM)] * 3
        + [pl.BlockSpec(memory_space=pl.ANY)],
        out_specs=pl.BlockSpec(memory_space=pl.ANY),
        scratch_shapes=[
            pltpu.VMEM(voltages.shape, bf16),
            pltpu.VMEM((TAPS, 8, NFFT), f32),
            pltpu.VMEM((2 * NFFT, 256), bf16),
            pltpu.VMEM((2, STEP * 8, NFFT), bf16),
            pltpu.VMEM((2, STEP * 8, 128), f32),
            pltpu.VMEM((2, 128 * 8, 128), f32),
            pltpu.VMEM((CHUNKS, chans, CMAX, 8, 2 * STEP), bf16),
            pltpu.VMEM((CHUNKS, chans, CMAX, 8, 2 * STEP), bf16),
            pltpu.VMEM((CHUNKS, stns, chans, 8, 2 * STEP), bf16),
            pltpu.VMEM(blocks, bf16),
            pltpu.VMEM((NSUB * ROOM, inputs) if packed else (16, 128), bf16),
            pltpu.VMEM((CHUNKS, NSUB * ROOM, 2 * STEP) if packed else (16, 128), bf16),
            pltpu.VMEM(blocks if packed else (8, 128), f32),
            pltpu.SemaphoreType.DMA((CHUNKS + 1,)),
            pltpu.SemaphoreType.DMA,
            pltpu.SemaphoreType.DMA((CHUNKS,)),
            pltpu.SemaphoreType.DMA,
            pltpu.SemaphoreType.DMA((CHUNKS,)),
            pltpu.SemaphoreType.DMA,
            pltpu.SemaphoreType.DMA,
        ],
        compiler_params=pltpu.CompilerParams(
            collective_id=1 if packed else 0, has_side_effects=True, vmem_limit_bytes=58 << 20
        ),
    )(band_start, band_count, fir_taps, target, member, voltages)


def place_kernel(in_ref, mask_ref, out_ref, scratch):
    mask = mask_ref[...]
    for q in range(CMAX):
        for o in range(2):
            values = in_ref[q, o].astype(f32) * mask
            for part in range(8):
                for half in range(2):
                    scratch[part, pl.ds(half * 256 + o * 16 + q, 8, stride=32), :] = values[
                        half * 8 : (half + 1) * 8, part * 128 : (part + 1) * 128
                    ]
    for part in range(8):
        out_ref[:, part * 128 : (part + 1) * 128] = scratch[part]


def place(blocks, mask):
    slots, _, rows, inputs = blocks.shape
    flat = pl.pallas_call(
        place_kernel,
        name="place",
        grid=(rows // 16,),
        out_shape=jax.ShapeDtypeStruct((rows * 2 * slots, inputs), f32),
        in_specs=[
            pl.BlockSpec((slots, 2, 16, inputs), lambda b: (0, 0, b, 0)),
            pl.BlockSpec((16, inputs), lambda b: (b, 0)),
        ],
        out_specs=pl.BlockSpec((16 * 2 * slots, inputs), lambda b: (b, 0)),
        scratch_shapes=[pltpu.VMEM((8, 16 * 2 * slots, 128), f32)],
        compiler_params=pltpu.CompilerParams(vmem_limit_bytes=60 << 20),
    )(blocks, mask)
    return flat.reshape(rows, 2, slots, inputs)


def unpack_kernel(in_ref, place_ref, mask_ref, out_ref, scratch, spread):
    slots, _, rows, room = in_ref.shape

    @pl.when(pl.program_id(0) == 0)
    def _():
        place = place_ref[...]
        row = lax.broadcasted_iota(jnp.int32, (room, place.shape[1]), 0)
        spread[...] = jnp.where(row == place, f32(1), f32(0)).astype(bf16)

    for q in range(slots):
        for o in range(2):
            values = in_ref[q, o].astype(f32)
            for part in range(room // 128):
                for half in range(rows // 8):
                    scratch[part, pl.ds(half * 256 + o * 16 + q, 8, stride=32), :] = values[
                        half * 8 : (half + 1) * 8, part * 128 : (part + 1) * 128
                    ]
    total = None
    for part in range(room // 128):
        product = jnp.dot(
            scratch[part].astype(bf16), spread[part * 128 : (part + 1) * 128, :],
            preferred_element_type=f32,
        )
        total = product if total is None else total + product
    for i in range(rows):
        out_ref[i * 32 : (i + 1) * 32, :] = total[i * 32 : (i + 1) * 32, :] * mask_ref[i : i + 1, :]


def unpack(blocks, placing, mask):
    slots, _, rows, room = blocks.shape
    inputs = mask.shape[1]
    flat = pl.pallas_call(
        unpack_kernel,
        name="unpack",
        grid=(rows // 16,),
        out_shape=jax.ShapeDtypeStruct((rows * 2 * slots, inputs), f32),
        in_specs=[
            pl.BlockSpec((slots, 2, 16, room), lambda b: (0, 0, b, 0)),
            pl.BlockSpec((1, inputs), lambda b: (0, 0)),
            pl.BlockSpec((16, inputs), lambda b: (b, 0)),
        ],
        out_specs=pl.BlockSpec((16 * 2 * slots, inputs), lambda b: (b, 0)),
        scratch_shapes=[
            pltpu.VMEM((room // 128, 16 * 2 * slots, 128), f32),
            pltpu.VMEM((room, inputs), bf16),
        ],
        compiler_params=pltpu.CompilerParams(vmem_limit_bytes=60 << 20),
    )(blocks, placing, mask)
    return flat.reshape(rows, 2, slots, inputs)


def per_device(voltages, fir_taps, band_start, band_count, subarray):
    inputs = 2 * subarray.shape[0]
    rows = inputs // lax.axis_size("stn")
    same = subarray[:, None] == subarray[None, :]
    index = jnp.arange(subarray.shape[0], dtype=jnp.int32)
    before = jnp.sum((same & (index[:, None] < index[None, :])).astype(jnp.int32), axis=0)
    fits = jnp.max(jnp.sum(same.astype(jnp.int32), axis=0)) <= ROOM // 2
    stations = jnp.repeat(subarray, 2)
    placing = jnp.repeat(2 * before, 2) + jnp.arange(inputs, dtype=jnp.int32) % 2
    target = (stations * ROOM + placing)[None, :]
    member = stations[:, None]
    own = lax.dynamic_slice_in_dim(stations, lax.axis_index("stn") * rows, rows, 0)
    mask = (own[:, None] == stations[None, :]).astype(f32) / SPECTRA

    def packed_way():
        blocks = correlator(True, voltages, fir_taps, band_start, band_count, target, member)
        return unpack(blocks, placing[None, :], mask)

    def full_way():
        blocks = correlator(False, voltages, fir_taps, band_start, band_count, target, member)
        return place(blocks, mask)

    return lax.cond(fits, packed_way, full_way)


def solution(mesh):
    in_specs = (P(None, ("stn", "chan"), None), P(), P(), P(), P())
    out_specs = P("stn", None, "chan", None)
    return jax.shard_map(
        per_device, mesh=mesh, in_specs=in_specs, out_specs=out_specs, check_vma=False
    )
```

```python
import functools
import math

import jax
import jax.numpy as jnp
from jax import lax
from jax.experimental import pallas as pl
from jax.experimental.pallas import tpu as pltpu
from jax.sharding import PartitionSpec as P

NFFT = 1024
TAPS = 12
HALF = TAPS // 2
SPECTRA = 512
CMAX = 16
GROUPS = 8
STEP = 64
CHUNKS = SPECTRA // STEP
PAIRS = CHUNKS // 2
ROOM = 320
MAIN = 256
REST = ROOM - MAIN
WIDE = MAIN + 2 * REST
NSUB = 4
f32 = jnp.float32
bf16 = jnp.bfloat16
MESH = pl.DeviceIdType.MESH
NT = (((1,), (1,)), ((), ()))


def fill_table(start_ref, count_ref, table):
    lane = lax.broadcasted_iota(jnp.int32, (8, 128), 1)
    channel = lane % CMAX
    scale = jnp.zeros((8, 128), f32)
    for g in range(GROUPS):
        here = lane // CMAX == g
        channel = jnp.where(here, channel + start_ref[g], channel)
        live = here & (lane % CMAX < count_ref[g])
        scale = jnp.where(live, f32(1.0 / math.sqrt(NFFT)), scale)
    row = lax.broadcasted_iota(jnp.int32, (8, 128), 0)

    def rows16(k, carry):
        cosines, sines = [], []
        for half in range(2):
            phase = ((row + (k * 16 + half * 8)) * channel) & (NFFT - 1)
            angle = phase.astype(f32) * f32(2.0 * math.pi / NFFT)
            cosines.append(jnp.cos(angle) * scale)
            sines.append(jnp.sin(angle) * scale)
        cosine = jnp.concatenate(cosines, 0).astype(bf16)
        sine = jnp.concatenate(sines, 0)
        top = pl.multiple_of(k * 16, 16)
        low = pl.multiple_of(NFFT + k * 16, 16)
        table[pl.ds(top, 16), 0:128] = cosine
        table[pl.ds(top, 16), 128:256] = (-sine).astype(bf16)
        table[pl.ds(low, 16), 0:128] = sine.astype(bf16)
        table[pl.ds(low, 16), 128:256] = cosine
        return carry

    lax.fori_loop(0, NFFT // 16, rows16, 0)


def weighted(values, weights):
    total = values[0] * weights[0]
    for value, weight in zip(values[1:], weights[1:]):
        total = total + value * weight
    return total


def filter_chunk(volt, taps8, frames, first):
    def strip(n, carry):
        part = n // 8
        column = (n % 8) * 128
        lanes = pl.ds(pl.multiple_of(column, 128), 128)
        taps = [taps8[p, :, lanes] for p in range(TAPS)]
        sums = [taps8[TAPS + q, :, lanes] for q in range(HALF)]

        def sample(j):
            start = pl.multiple_of((first + j) * NFFT + column, 128)
            return volt[part, :, pl.ds(start, 128)].astype(f32)

        evens = [sample(2 * q) for q in range(HALF)]
        odds = [sample(2 * q + 1) for q in range(HALF - 1)]
        both = [e + o for e, o in zip(evens, odds)]
        b_now = weighted(evens, taps[1::2])
        for k in range(STEP // 2):
            odds.append(sample(2 * (k + HALF) - 1))
            both.append(evens[-1] + odds[-1])
            a_now = weighted(odds, taps[0::2])
            c_now = weighted(both, sums)
            evens = evens[1:] + [sample(2 * (k + HALF))]
            b_next = weighted(evens, taps[1::2])
            out = jnp.concatenate([c_now - (a_now + b_now), a_now + b_next], 0)
            frames[part, k * 16 : (k + 1) * 16, lanes] = out.astype(bf16)
            b_now = b_next
            odds = odds[1:]
            both = both[1:]
        return carry

    lax.fori_loop(0, 2 * NFFT // 128, strip, 0)


def transform_chunk(frames, table, mixed):
    product = jnp.dot(frames[0], table[0:NFFT, :], preferred_element_type=f32)
    product = product + jnp.dot(frames[1], table[NFFT:, :], preferred_element_type=f32)
    for o in range(2):
        mixed[o] = product[:, o * 128 : (o + 1) * 128]


def sort_chunk(mixed, sorted_, outgoing, c):
    for i in range(8):
        both = jnp.concatenate([mixed[o, pl.ds(i, STEP, stride=8), :] for o in range(2)], axis=0)
        sorted_[pl.ds(i, 128, stride=8), :] = both.T
    outgoing[c] = sorted_[...].reshape(outgoing.shape[1:]).astype(bf16)


def rank_members(stations, picker):
    inputs = stations.shape[1]

    def rows16(k, carry):
        top = pl.multiple_of(k * 16, 16)
        row = lax.broadcasted_iota(jnp.int32, (16, inputs), 0) + top
        column = lax.broadcasted_iota(jnp.int32, (16, inputs), 1)
        picker[pl.ds(top, 16), :] = jnp.where(row < column, f32(1), f32(0)).astype(bf16)
        return carry

    lax.fori_loop(0, inputs // 16, rows16, 0)
    kind = lax.broadcasted_iota(jnp.int32, (16, inputs), 0).astype(f32)
    onehot = jnp.where(kind == stations, f32(1), f32(0))
    before = jnp.dot(onehot.astype(bf16), picker[0:inputs, :], preferred_element_type=f32)
    return jnp.sum(onehot * before, axis=0, keepdims=True)


def fill_picker(target, picker):
    def rows16(k, carry):
        top = pl.multiple_of(k * 16, 16)
        column = top % WIDE
        base = (top // WIDE) * ROOM + column - jnp.where(column >= ROOM, REST, 0)
        row = lax.broadcasted_iota(jnp.int32, (16, target.shape[1]), 0) + base
        picker[pl.ds(top, 16), :] = jnp.where(row.astype(f32) == target, f32(1), f32(0)).astype(bf16)
        return carry

    lax.fori_loop(0, NSUB * WIDE // 16, rows16, 0)


def fill_turn(turn):
    row = lax.broadcasted_iota(jnp.int32, turn.shape, 0)
    column = lax.broadcasted_iota(jnp.int32, turn.shape, 1)
    low = column % (2 * STEP) < STEP
    ones = jnp.where(low & (row == column + STEP), f32(1), f32(0))
    turn[...] = (ones - jnp.where(~low & (row == column - STEP), f32(1), f32(0))).astype(bf16)


def total_wait(ref, sem):
    pltpu.make_async_copy(ref, ref, sem).wait()


def correlator_kernel(
    packed, start_ref, count_ref, taps_ref, stations_ref, volt_hbm, out_ref, placing_ref,
    volt, taps8, table, frames, mixed, sorted_, outgoing, passing, held, results,
    turn, picker, member, picked, summed, volt_sem, send_a, recv_a, send_b, recv_b, send_c, recv_c,
):
    chan, stn = lax.axis_index("chan"), lax.axis_index("stn")
    chans, stns = lax.axis_size("chan"), lax.axis_size("stn")

    def volt_copy(c, first):
        low = first * NFFT
        wide = STEP * NFFT
        span = pl.ds(pl.multiple_of(low, 128), wide)
        return pltpu.make_async_copy(volt_hbm.at[:, :, span], volt.at[:, :, span], volt_sem.at[c])

    halo = pl.ds(SPECTRA * NFFT, (TAPS - 1) * NFFT)
    halo_copy = pltpu.make_async_copy(volt_hbm.at[:, :, halo], volt.at[:, :, halo], volt_sem.at[CHUNKS])
    for c in range(CHUNKS):
        volt_copy(c, c * STEP).start()
    halo_copy.start()

    barrier = pltpu.get_barrier_semaphore()
    for d in range(1, chans):
        pl.semaphore_signal(barrier, inc=1, device_id=((chan + d) % chans, stn), device_id_type=MESH)
    for d in range(1, stns):
        pl.semaphore_signal(barrier, inc=1, device_id=(chan, (stn + d) % stns), device_id_type=MESH)

    for p in range(TAPS):
        taps8[p] = jnp.broadcast_to(taps_ref[p : p + 1, :], (8, NFFT))
    for q in range(HALF):
        taps8[TAPS + q] = taps8[2 * q] + taps8[2 * q + 1]
    fill_table(start_ref, count_ref, table)
    pl.semaphore_wait(barrier, chans + stns - 2)

    def send_chan(c):
        for d in range(1, chans):
            to = (chan + d) % chans
            pltpu.make_async_remote_copy(
                outgoing.at[c, to], passing.at[c, chan], send_a, recv_a.at[c],
                device_id=(to, stn), device_id_type=MESH,
            ).start()
        pltpu.make_async_copy(outgoing.at[c, chan], passing.at[c, chan], recv_a.at[c]).start()

    def held_part(c):
        half = pl.ds(pl.multiple_of((c % 2) * 2 * STEP, 128), 2 * STEP)
        return held.at[c // 2, :, :, :, half]

    def send_stn(c):
        total_wait(passing.at[c], recv_a.at[c])
        for d in range(1, stns):
            to = (stn + d) % stns
            pltpu.make_async_remote_copy(
                passing.at[c, :, to], held_part(c).at[stn], send_b, recv_b.at[c],
                device_id=(chan, to), device_id_type=MESH,
            ).start()
        pltpu.make_async_copy(passing.at[c, :, stn], held_part(c).at[stn], recv_b.at[c]).start()

    volt_copy(0, 0).wait()

    def chunk(c, carry):
        @pl.when(c < CHUNKS - 1)
        def _():
            volt_copy(c + 1, (c + 1) * STEP).wait()

        @pl.when(c == CHUNKS - 1)
        def _():
            halo_copy.wait()

        filter_chunk(volt, taps8, frames, c * STEP)
        transform_chunk(frames, table, mixed)
        sort_chunk(mixed, sorted_, outgoing, c)
        send_chan(c)

        @pl.when(c > 1)
        def _():
            send_stn(c - 2)

        return carry

    lax.fori_loop(0, CHUNKS, chunk, 0)
    fill_turn(turn)
    if packed:
        stations = stations_ref[...]
        placing = rank_members(stations, picker)
        placing_ref[...] = placing
        fill_picker(stations * ROOM + placing, picker)
        for b in range(stations.shape[1] // 128):
            strip = jnp.broadcast_to(stations[:, b * 128 : (b + 1) * 128], (128, 128))
            member[b * 128 : (b + 1) * 128, :] = strip.T
    else:
        placing_ref[...] = jnp.zeros_like(placing_ref)
    send_stn(CHUNKS - 2)

    inputs = stns * chans * 8
    rows = chans * 8
    quad = 4

    def arrived(c):
        for half in range(2):
            total_wait(held.at[c, :, :, :, 0 : 2 * STEP], recv_b.at[2 * c + half])

    def pick(c):
        arrived(c)
        everyone = held[c].reshape(inputs, 4 * STEP)
        picked[c] = jnp.dot(picker[...], everyone, preferred_element_type=f32).astype(bf16)

    def add_up(c, b):
        own = held[c, pl.ds(b * quad, quad)].reshape(quad * rows, 4 * STEP)
        turned = jnp.dot(own, turn[...], preferred_element_type=f32).astype(bf16)
        both = jnp.concatenate([own, turned], axis=0)
        product = lax.dot_general(both, picked[c], NT, preferred_element_type=f32)
        kinds = member[pl.ds(pl.multiple_of(b * quad * rows, 8), quad * rows), :]
        kinds = jnp.concatenate([kinds] * (WIDE // 128), axis=1)
        parts = []
        for o in range(2):
            wide = product[o * quad * rows : (o + 1) * quad * rows]
            chosen = wide[:, 0:WIDE]
            for n in range(1, NSUB):
                chosen = jnp.where(kinds == n, wide[:, n * WIDE : (n + 1) * WIDE], chosen)
            if c > 0:
                chosen = chosen + summed[b, o]
            if c < PAIRS - 1:
                summed[b, o] = chosen
            parts.append(chosen)
        if c == PAIRS - 1:
            lane = lax.broadcasted_iota(jnp.int32, (quad * rows, 2 * REST), 1)
            rest = jnp.where(lane < REST, parts[0][:, MAIN:], parts[1][:, MAIN:])
            full = jnp.concatenate([parts[0][:, :MAIN], parts[1][:, :MAIN], rest], axis=1)
            results[pl.ds(b * quad, quad)] = full.astype(bf16).reshape(quad, rows, 2 * ROOM)

    def return_rows(k):
        @pl.when(k != stn)
        def _():
            pltpu.make_async_remote_copy(
                results.at[k], out_ref.at[stn], send_c, recv_c,
                device_id=(chan, k), device_id_type=MESH,
            ).start()

        @pl.when(k == stn)
        def _():
            pltpu.make_async_copy(results.at[k], out_ref.at[stn], recv_c).start()

    def add_pair(c):
        pick(c)

        def add_block(s, carry):
            b = (stn // quad + 1 + s) % (stns // quad)
            add_up(c, b)
            if c == PAIRS - 1:
                for e in range(quad):
                    return_rows(b * quad + e)
            return carry

        lax.fori_loop(0, stns // quad, add_block, 0)

    if packed:
        add_pair(0)
        send_stn(CHUNKS - 1)
        for c in range(1, PAIRS):
            add_pair(c)
    else:
        send_stn(CHUNKS - 1)
        for c in range(PAIRS):
            arrived(c)

    def correlate(s, carry):
        k = (stn + 7 * (s + 1)) % stns
        total = None
        for c in range(PAIRS):
            own = held[c, k].reshape(rows, 4 * STEP)
            turned = jnp.dot(own, turn[...], preferred_element_type=f32).astype(bf16)
            both = jnp.concatenate([own, turned], axis=0)
            part = lax.dot_general(
                both, held[c].reshape(inputs, 4 * STEP), NT, preferred_element_type=f32
            )
            total = part if total is None else total + part
        results[k] = total.reshape(2, rows, inputs).astype(bf16)

        return_rows(k)
        return carry

    if not packed:
        lax.fori_loop(0, stns, correlate, 0)
    total_wait(outgoing.at[:, 0 : chans - 1], send_a)
    total_wait(held.at[:, 0 : stns - 1], send_b)
    total_wait(results.at[0 : stns - 1], send_c)
    total_wait(out_ref, recv_c)


def correlator(packed, voltages, fir_taps, band_start, band_count, stations):
    chans, stns = lax.axis_size("chan"), lax.axis_size("stn")
    inputs = stns * chans * 8
    blocks = (stns, chans * 8, 2 * ROOM) if packed else (stns, 2, chans * 8, inputs)
    sums = (stns // 4, 2, chans * 32, WIDE)
    return pl.pallas_call(
        functools.partial(correlator_kernel, packed),
        name="correlator_packed" if packed else "correlator",
        out_shape=(
            jax.ShapeDtypeStruct(blocks, bf16),
            jax.ShapeDtypeStruct((1, inputs), f32),
        ),
        in_specs=[pl.BlockSpec(memory_space=pltpu.SMEM)] * 2
        + [pl.BlockSpec(memory_space=pltpu.VMEM)] * 2
        + [pl.BlockSpec(memory_space=pl.ANY)],
        out_specs=(pl.BlockSpec(memory_space=pl.ANY), pl.BlockSpec(memory_space=pltpu.VMEM)),
        scratch_shapes=[
            pltpu.VMEM(voltages.shape, bf16),
            pltpu.VMEM((TAPS + HALF, 8, NFFT), f32),
            pltpu.VMEM((2 * NFFT, 256), bf16),
            pltpu.VMEM((2, STEP * 8, NFFT), bf16),
            pltpu.VMEM((2, STEP * 8, 128), f32),
            pltpu.VMEM((128 * 8, 128), f32),
            pltpu.VMEM((CHUNKS, chans, CMAX, 8, 2 * STEP), bf16),
            pltpu.VMEM((CHUNKS, chans, CMAX, 8, 2 * STEP), bf16),
            pltpu.VMEM((PAIRS, stns, chans, 8, 4 * STEP), bf16),
            pltpu.VMEM(blocks, bf16),
            pltpu.VMEM((4 * STEP, 4 * STEP), bf16),
            pltpu.VMEM((NSUB * WIDE, inputs) if packed else (16, 128), bf16),
            pltpu.VMEM((inputs, 128) if packed else (8, 128), f32),
            pltpu.VMEM((PAIRS, NSUB * WIDE, 4 * STEP) if packed else (16, 128), bf16),
            pltpu.VMEM(sums if packed else (8, 128), f32),
            pltpu.SemaphoreType.DMA((CHUNKS + 1,)),
            pltpu.SemaphoreType.DMA,
            pltpu.SemaphoreType.DMA((CHUNKS,)),
            pltpu.SemaphoreType.DMA,
            pltpu.SemaphoreType.DMA((CHUNKS,)),
            pltpu.SemaphoreType.DMA,
            pltpu.SemaphoreType.DMA,
        ],
        compiler_params=pltpu.CompilerParams(
            collective_id=1 if packed else 0, has_side_effects=True, vmem_limit_bytes=58 << 20
        ),
    )(band_start, band_count, fir_taps, stations, voltages)


def place_kernel(in_ref, mask_ref, out_ref, scratch):
    mask = mask_ref[...]
    for q in range(CMAX):
        for o in range(2):
            values = in_ref[q, o].astype(f32) * mask
            for part in range(8):
                for half in range(2):
                    scratch[part, pl.ds(half * 256 + o * 16 + q, 8, stride=32), :] = values[
                        half * 8 : (half + 1) * 8, part * 128 : (part + 1) * 128
                    ]
    for part in range(8):
        out_ref[:, part * 128 : (part + 1) * 128] = scratch[part]


def place(blocks, mask):
    slots, _, rows, inputs = blocks.shape
    flat = pl.pallas_call(
        place_kernel,
        name="place",
        grid=(rows // 16,),
        out_shape=jax.ShapeDtypeStruct((rows * 2 * slots, inputs), f32),
        in_specs=[
            pl.BlockSpec((slots, 2, 16, inputs), lambda b: (0, 0, b, 0)),
            pl.BlockSpec((16, inputs), lambda b: (b, 0)),
        ],
        out_specs=pl.BlockSpec((16 * 2 * slots, inputs), lambda b: (b, 0)),
        scratch_shapes=[pltpu.VMEM((8, 16 * 2 * slots, 128), f32)],
        compiler_params=pltpu.CompilerParams(vmem_limit_bytes=60 << 20),
    )(blocks, mask)
    return flat.reshape(rows, 2, slots, inputs)


def unpack_kernel(own_ref, in_ref, place_ref, stations_ref, out_ref, scratch, spread):
    slots, rows, _ = in_ref.shape

    @pl.when(pl.program_id(0) == 0)
    def _():
        place = place_ref[...]
        row = lax.broadcasted_iota(jnp.int32, (WIDE, place.shape[1]), 0)
        for o in range(2):
            mine = (row < MAIN) | ((row >= MAIN + o * REST) & (row < ROOM + o * REST))
            rank = jnp.where(mine, jnp.where(row < MAIN, row, row - o * REST), -1)
            spread[o] = jnp.where(rank.astype(f32) == place, f32(1), f32(0)).astype(bf16)

    for q in range(slots):
        values = in_ref[q].astype(f32)
        for part in range(2 * ROOM // 128):
            for half in range(rows // 8):
                scratch[part, pl.ds(half * 8 * slots + q, 8, stride=slots), :] = values[
                    half * 8 : (half + 1) * 8, part * 128 : (part + 1) * 128
                ]
    stations = stations_ref[...]
    masks = []
    for i in range(rows // 2):
        kind = own_ref[pl.program_id(0) * (rows // 2) + i].astype(f32)
        masks.append(jnp.where(stations == kind, f32(1.0 / SPECTRA), f32(0)))
    for o in range(2):
        packed = [scratch[part].astype(bf16) for part in (2 * o, 2 * o + 1, 4)]
        total = jnp.dot(jnp.concatenate(packed, axis=1), spread[o], preferred_element_type=f32)
        for i in range(rows):
            out_ref[i, o] = total[i * slots : (i + 1) * slots, :] * masks[i // 2]


def unpack(blocks, placing, stations, own):
    slots, rows, _ = blocks.shape
    inputs = stations.shape[1]
    return pl.pallas_call(
        unpack_kernel,
        name="unpack",
        grid=(rows // 16,),
        out_shape=jax.ShapeDtypeStruct((rows, 2, slots, inputs), f32),
        in_specs=[
            pl.BlockSpec(memory_space=pltpu.SMEM),
            pl.BlockSpec((slots, 16, 2 * ROOM), lambda b: (0, b, 0)),
            pl.BlockSpec((1, inputs), lambda b: (0, 0)),
            pl.BlockSpec((1, inputs), lambda b: (0, 0)),
        ],
        out_specs=pl.BlockSpec((16, 2, slots, inputs), lambda b: (b, 0, 0, 0)),
        scratch_shapes=[
            pltpu.VMEM((2 * ROOM // 128, 16 * slots, 128), f32),
            pltpu.VMEM((2, WIDE, inputs), bf16),
        ],
        compiler_params=pltpu.CompilerParams(vmem_limit_bytes=60 << 20),
    )(own, blocks, placing, stations)


def per_device(voltages, fir_taps, band_start, band_count, subarray):
    count = subarray.shape[0] // lax.axis_size("stn")
    kinds = jnp.arange(NSUB, dtype=jnp.int32)
    sizes = jnp.sum((subarray[None, :] == kinds[:, None]).astype(jnp.int32), axis=1)
    fits = jnp.max(sizes) <= ROOM // 2
    own = lax.dynamic_slice_in_dim(subarray, lax.axis_index("stn") * count, count, 0)
    stations = jnp.repeat(subarray.astype(f32), 2)[None, :]

    def packed_way():
        blocks, placing = correlator(True, voltages, fir_taps, band_start, band_count, stations)
        return unpack(blocks, placing, stations, own)

    def full_way():
        blocks, _ = correlator(False, voltages, fir_taps, band_start, band_count, stations)
        own_rows = jnp.repeat(own, 2)[:, None].astype(f32)
        return place(blocks, (own_rows == stations).astype(f32) / SPECTRA)

    return lax.cond(fits, packed_way, full_way)


def solution(mesh):
    in_specs = (P(None, ("stn", "chan"), None), P(), P(), P(), P())
    out_specs = P("stn", None, "chan", None)
    return jax.shard_map(
        per_device, mesh=mesh, in_specs=in_specs, out_specs=out_specs, check_vma=False
    )
```

```python
import functools
import math

import jax
import jax.numpy as jnp
from jax import lax
from jax.experimental import pallas as pl
from jax.experimental.pallas import tpu as pltpu
from jax.sharding import PartitionSpec as P

NFFT = 1024
TAPS = 12
HALF = TAPS // 2
SPECTRA = 512
CMAX = 16
GROUPS = 8
STEP = 64
CHUNKS = SPECTRA // STEP
PAIRS = CHUNKS // 2
ROOM = 320
MAIN = 256
REST = ROOM - MAIN
WIDE = MAIN + 2 * REST
NSUB = 4
f32 = jnp.float32
bf16 = jnp.bfloat16
MESH = pl.DeviceIdType.MESH
NT = (((1,), (1,)), ((), ()))


def fill_table(start_ref, count_ref, table):
    lane = lax.broadcasted_iota(jnp.int32, (8, 128), 1)
    channel = lane % CMAX
    scale = jnp.zeros((8, 128), f32)
    for g in range(GROUPS):
        here = lane // CMAX == g
        channel = jnp.where(here, channel + start_ref[g], channel)
        live = here & (lane % CMAX < count_ref[g])
        scale = jnp.where(live, f32(1.0 / math.sqrt(NFFT)), scale)
    row = lax.broadcasted_iota(jnp.int32, (8, 128), 0)

    def rows16(k, carry):
        cosines, sines = [], []
        for half in range(2):
            phase = ((row + (k * 16 + half * 8)) * channel) & (NFFT - 1)
            angle = phase.astype(f32) * f32(2.0 * math.pi / NFFT)
            cosines.append(jnp.cos(angle) * scale)
            sines.append(jnp.sin(angle) * scale)
        cosine = jnp.concatenate(cosines, 0).astype(bf16)
        sine = jnp.concatenate(sines, 0)
        top = pl.multiple_of(k * 16, 16)
        low = pl.multiple_of(NFFT + k * 16, 16)
        table[pl.ds(top, 16), 0:128] = cosine
        table[pl.ds(top, 16), 128:256] = (-sine).astype(bf16)
        table[pl.ds(low, 16), 0:128] = sine.astype(bf16)
        table[pl.ds(low, 16), 128:256] = cosine
        return carry

    lax.fori_loop(0, NFFT // 16, rows16, 0)


def weighted(values, weights):
    total = values[0] * weights[0]
    for value, weight in zip(values[1:], weights[1:]):
        total = total + value * weight
    return total


def once(function):
    known = {}

    def get(k):
        if k not in known:
            known[k] = function(k)
        return known[k]

    return get


def halved(stream, taps, sums):
    reach = range(len(sums))
    odds = lambda m: stream(2 * m + 1)
    evens = lambda m: stream(2 * m)
    both = once(lambda m: evens(m) + odds(m))
    a = once(lambda m: weighted([odds(m + q) for q in reach], taps[0::2]))
    b = once(lambda m: weighted([evens(m + q) for q in reach], taps[1::2]))
    c = once(lambda m: weighted([both(m + q) for q in reach], sums))

    def output(k):
        m = k // 2
        return c(m) - (a(m) + b(m)) if k % 2 == 0 else a(m) + b(m + 1)

    return once(output)


def filter_chunk(volt, taps8, frames, first):
    def strip(n, carry):
        part = n // 8
        column = (n % 8) * 128
        lanes = pl.ds(pl.multiple_of(column, 128), 128)
        taps = [taps8[p, :, lanes] for p in range(TAPS + 5 * HALF // 2)]

        def sample(j):
            start = pl.multiple_of((first + j) * NFFT + column, 128)
            return volt[part, :, pl.ds(start, 128)].astype(f32)

        odds = once(lambda k: sample(2 * k + 1))
        evens = once(lambda k: sample(2 * k))
        both = once(lambda k: evens(k) + odds(k))
        third = HALF // 2
        a = halved(odds, taps[0:TAPS:2], taps[TAPS + HALF : TAPS + HALF + third])
        b = halved(evens, taps[1:TAPS:2], taps[TAPS + HALF + third : TAPS + HALF + 2 * third])
        c = halved(both, taps[TAPS : TAPS + HALF], taps[TAPS + HALF + 2 * third :])
        for k in range(STEP // 2):
            out = jnp.concatenate([c(k) - (a(k) + b(k)), a(k) + b(k + 1)], 0)
            frames[k * 16 : (k + 1) * 16, pl.ds(pl.multiple_of(n * 128, 128), 128)] = out.astype(bf16)
        return carry

    lax.fori_loop(0, 2 * NFFT // 128, strip, 0)


def transform_chunk(frames, table, mixed):
    product = jnp.dot(frames[...], table[...], preferred_element_type=f32)
    for o in range(2):
        mixed[o] = product[:, o * 128 : (o + 1) * 128]


def sort_chunk(mixed, sorted_, outgoing, c):
    for i in range(8):
        both = jnp.concatenate([mixed[o, pl.ds(i, STEP, stride=8), :] for o in range(2)], axis=0)
        sorted_[pl.ds(i, 128, stride=8), :] = both.T
    outgoing[c] = sorted_[...].reshape(outgoing.shape[1:]).astype(bf16)


def rank_members(stations, picker):
    inputs = stations.shape[1]

    def rows16(k, carry):
        top = pl.multiple_of(k * 16, 16)
        row = lax.broadcasted_iota(jnp.int32, (16, inputs), 0) + top
        column = lax.broadcasted_iota(jnp.int32, (16, inputs), 1)
        picker[pl.ds(top, 16), :] = jnp.where(row < column, f32(1), f32(0)).astype(bf16)
        return carry

    lax.fori_loop(0, inputs // 16, rows16, 0)
    kind = lax.broadcasted_iota(jnp.int32, (16, inputs), 0).astype(f32)
    onehot = jnp.where(kind == stations, f32(1), f32(0))
    before = jnp.dot(onehot.astype(bf16), picker[0:inputs, :], preferred_element_type=f32)
    return jnp.sum(onehot * before, axis=0, keepdims=True)


def fill_picker(target, picker):
    def rows16(k, carry):
        top = pl.multiple_of(k * 16, 16)
        column = top % WIDE
        base = (top // WIDE) * ROOM + column - jnp.where(column >= ROOM, REST, 0)
        row = lax.broadcasted_iota(jnp.int32, (16, target.shape[1]), 0) + base
        picker[pl.ds(top, 16), :] = jnp.where(row.astype(f32) == target, f32(1), f32(0)).astype(bf16)
        return carry

    lax.fori_loop(0, NSUB * WIDE // 16, rows16, 0)


def fill_turn(turn):
    row = lax.broadcasted_iota(jnp.int32, turn.shape, 0)
    column = lax.broadcasted_iota(jnp.int32, turn.shape, 1)
    low = column % (2 * STEP) < STEP
    ones = jnp.where(low & (row == column + STEP), f32(1), f32(0))
    turn[...] = (ones - jnp.where(~low & (row == column - STEP), f32(1), f32(0))).astype(bf16)


def total_wait(ref, sem):
    pltpu.make_async_copy(ref, ref, sem).wait()


def correlator_kernel(
    packed, start_ref, count_ref, taps_ref, stations_ref, volt_hbm, out_ref, placing_ref,
    volt, taps8, table, frames, mixed, sorted_, outgoing, passing, held, results,
    turn, picker, member, picked, summed, volt_sem, send_a, recv_a, send_b, recv_b, send_c, recv_c,
):
    chan, stn = lax.axis_index("chan"), lax.axis_index("stn")
    chans, stns = lax.axis_size("chan"), lax.axis_size("stn")

    def volt_copy(c, first):
        low = first * NFFT
        wide = STEP * NFFT
        span = pl.ds(pl.multiple_of(low, 128), wide)
        return pltpu.make_async_copy(volt_hbm.at[:, :, span], volt.at[:, :, span], volt_sem.at[c])

    halo = pl.ds(SPECTRA * NFFT, (TAPS - 1) * NFFT)
    halo_copy = pltpu.make_async_copy(volt_hbm.at[:, :, halo], volt.at[:, :, halo], volt_sem.at[CHUNKS])
    for c in range(CHUNKS):
        volt_copy(c, c * STEP).start()
    halo_copy.start()

    barrier = pltpu.get_barrier_semaphore()
    for d in range(1, chans):
        pl.semaphore_signal(barrier, inc=1, device_id=((chan + d) % chans, stn), device_id_type=MESH)
    for d in range(1, stns):
        pl.semaphore_signal(barrier, inc=1, device_id=(chan, (stn + d) % stns), device_id_type=MESH)

    for p in range(TAPS):
        taps8[p] = jnp.broadcast_to(taps_ref[p : p + 1, :], (8, NFFT))
    for q in range(HALF):
        taps8[TAPS + q] = taps8[2 * q] + taps8[2 * q + 1]
    third = HALF // 2
    for q in range(third):
        low, high = TAPS + 2 * q, TAPS + 2 * q + 1
        taps8[TAPS + HALF + q] = taps8[4 * q] + taps8[4 * q + 2]
        taps8[TAPS + HALF + third + q] = taps8[4 * q + 1] + taps8[4 * q + 3]
        taps8[TAPS + HALF + 2 * third + q] = taps8[low] + taps8[high]
    fill_table(start_ref, count_ref, table)
    pl.semaphore_wait(barrier, chans + stns - 2)

    def send_chan(c):
        for d in range(1, chans):
            to = (chan + d) % chans
            pltpu.make_async_remote_copy(
                outgoing.at[c, to], passing.at[c, chan], send_a, recv_a.at[c],
                device_id=(to, stn), device_id_type=MESH,
            ).start()
        pltpu.make_async_copy(outgoing.at[c, chan], passing.at[c, chan], recv_a.at[c]).start()

    def held_part(c):
        half = pl.ds(pl.multiple_of((c % 2) * 2 * STEP, 128), 2 * STEP)
        return held.at[c // 2, :, :, :, half]

    def send_stn(c):
        total_wait(passing.at[c], recv_a.at[c])
        for d in range(1, stns):
            to = (stn + d) % stns
            pltpu.make_async_remote_copy(
                passing.at[c, :, to], held_part(c).at[stn], send_b, recv_b.at[c],
                device_id=(chan, to), device_id_type=MESH,
            ).start()
        pltpu.make_async_copy(passing.at[c, :, stn], held_part(c).at[stn], recv_b.at[c]).start()

    volt_copy(0, 0).wait()

    def chunk(c, carry):
        @pl.when(c < CHUNKS - 1)
        def _():
            volt_copy(c + 1, (c + 1) * STEP).wait()

        @pl.when(c == CHUNKS - 1)
        def _():
            halo_copy.wait()

        filter_chunk(volt, taps8, frames, c * STEP)
        transform_chunk(frames, table, mixed)
        sort_chunk(mixed, sorted_, outgoing, c)
        send_chan(c)

        @pl.when(c > 1)
        def _():
            send_stn(c - 2)

        return carry

    lax.fori_loop(0, CHUNKS, chunk, 0)
    fill_turn(turn)
    if packed:
        stations = stations_ref[...]
        placing = rank_members(stations, picker)
        placing_ref[...] = placing
        fill_picker(stations * ROOM + placing, picker)
        for b in range(stations.shape[1] // 128):
            strip = jnp.broadcast_to(stations[:, b * 128 : (b + 1) * 128], (128, 128))
            member[b * 128 : (b + 1) * 128, :] = strip.T
    else:
        placing_ref[...] = jnp.zeros_like(placing_ref)
    send_stn(CHUNKS - 2)

    inputs = stns * chans * 8
    rows = chans * 8
    quad = 4

    def arrived(c):
        for half in range(2):
            total_wait(held.at[c, :, :, :, 0 : 2 * STEP], recv_b.at[2 * c + half])

    def pick(c):
        arrived(c)
        everyone = held[c].reshape(inputs, 4 * STEP)
        picked[c] = jnp.dot(picker[...], everyone, preferred_element_type=f32).astype(bf16)

    def add_up(c, b):
        own = held[c, pl.ds(b * quad, quad)].reshape(quad * rows, 4 * STEP)
        turned = jnp.dot(own, turn[...], preferred_element_type=f32).astype(bf16)
        both = jnp.concatenate([own, turned], axis=0)
        product = lax.dot_general(both, picked[c], NT, preferred_element_type=f32)
        kinds = member[pl.ds(pl.multiple_of(b * quad * rows, 8), quad * rows), :]
        kinds = jnp.concatenate([kinds] * (WIDE // 128), axis=1)
        parts = []
        for o in range(2):
            wide = product[o * quad * rows : (o + 1) * quad * rows]
            chosen = wide[:, 0:WIDE]
            for n in range(1, NSUB):
                chosen = jnp.where(kinds == n, wide[:, n * WIDE : (n + 1) * WIDE], chosen)
            if c > 0:
                chosen = chosen + summed[b, o]
            if c < PAIRS - 1:
                summed[b, o] = chosen
            parts.append(chosen)
        if c == PAIRS - 1:
            lane = lax.broadcasted_iota(jnp.int32, (quad * rows, 2 * REST), 1)
            rest = jnp.where(lane < REST, parts[0][:, MAIN:], parts[1][:, MAIN:])
            full = jnp.concatenate([parts[0][:, :MAIN], parts[1][:, :MAIN], rest], axis=1)
            results[pl.ds(b * quad, quad)] = full.astype(bf16).reshape(quad, rows, 2 * ROOM)

    def return_rows(k):
        @pl.when(k != stn)
        def _():
            pltpu.make_async_remote_copy(
                results.at[k], out_ref.at[stn], send_c, recv_c,
                device_id=(chan, k), device_id_type=MESH,
            ).start()

        @pl.when(k == stn)
        def _():
            pltpu.make_async_copy(results.at[k], out_ref.at[stn], recv_c).start()

    def add_pair(c):
        pick(c)

        def add_block(s, carry):
            b = (stn // quad + 1 + s) % (stns // quad)
            add_up(c, b)
            if c == PAIRS - 1:
                for e in range(quad):
                    return_rows(b * quad + e)
            return carry

        lax.fori_loop(0, stns // quad, add_block, 0)

    if packed:
        add_pair(0)
        send_stn(CHUNKS - 1)
        for c in range(1, PAIRS):
            add_pair(c)
    else:
        send_stn(CHUNKS - 1)
        for c in range(PAIRS):
            arrived(c)

    def correlate(s, carry):
        k = (stn + 7 * (s + 1)) % stns
        total = None
        for c in range(PAIRS):
            own = held[c, k].reshape(rows, 4 * STEP)
            turned = jnp.dot(own, turn[...], preferred_element_type=f32).astype(bf16)
            both = jnp.concatenate([own, turned], axis=0)
            part = lax.dot_general(
                both, held[c].reshape(inputs, 4 * STEP), NT, preferred_element_type=f32
            )
            total = part if total is None else total + part
        results[k] = total.reshape(2, rows, inputs).astype(bf16)

        return_rows(k)
        return carry

    if not packed:
        lax.fori_loop(0, stns, correlate, 0)
    total_wait(outgoing.at[:, 0 : chans - 1], send_a)
    total_wait(held.at[:, 0 : stns - 1], send_b)
    total_wait(results.at[0 : stns - 1], send_c)
    total_wait(out_ref, recv_c)


def correlator(packed, voltages, fir_taps, band_start, band_count, stations):
    chans, stns = lax.axis_size("chan"), lax.axis_size("stn")
    inputs = stns * chans * 8
    blocks = (stns, chans * 8, 2 * ROOM) if packed else (stns, 2, chans * 8, inputs)
    sums = (stns // 4, 2, chans * 32, WIDE)
    return pl.pallas_call(
        functools.partial(correlator_kernel, packed),
        name="correlator_packed" if packed else "correlator",
        out_shape=(
            jax.ShapeDtypeStruct(blocks, bf16),
            jax.ShapeDtypeStruct((1, inputs), f32),
        ),
        in_specs=[pl.BlockSpec(memory_space=pltpu.SMEM)] * 2
        + [pl.BlockSpec(memory_space=pltpu.VMEM)] * 2
        + [pl.BlockSpec(memory_space=pl.ANY)],
        out_specs=(pl.BlockSpec(memory_space=pl.ANY), pl.BlockSpec(memory_space=pltpu.VMEM)),
        scratch_shapes=[
            pltpu.VMEM(voltages.shape, bf16),
            pltpu.VMEM((TAPS + 5 * HALF // 2, 8, NFFT), f32),
            pltpu.VMEM((2 * NFFT, 256), bf16),
            pltpu.VMEM((STEP * 8, 2 * NFFT), bf16),
            pltpu.VMEM((2, STEP * 8, 128), f32),
            pltpu.VMEM((128 * 8, 128), f32),
            pltpu.VMEM((CHUNKS, chans, CMAX, 8, 2 * STEP), bf16),
            pltpu.VMEM((CHUNKS, chans, CMAX, 8, 2 * STEP), bf16),
            pltpu.VMEM((PAIRS, stns, chans, 8, 4 * STEP), bf16),
            pltpu.VMEM(blocks, bf16),
            pltpu.VMEM((4 * STEP, 4 * STEP), bf16),
            pltpu.VMEM((NSUB * WIDE, inputs) if packed else (16, 128), bf16),
            pltpu.VMEM((inputs, 128) if packed else (8, 128), f32),
            pltpu.VMEM((PAIRS, NSUB * WIDE, 4 * STEP) if packed else (16, 128), bf16),
            pltpu.VMEM(sums if packed else (8, 128), f32),
            pltpu.SemaphoreType.DMA((CHUNKS + 1,)),
            pltpu.SemaphoreType.DMA,
            pltpu.SemaphoreType.DMA((CHUNKS,)),
            pltpu.SemaphoreType.DMA,
            pltpu.SemaphoreType.DMA((CHUNKS,)),
            pltpu.SemaphoreType.DMA,
            pltpu.SemaphoreType.DMA,
        ],
        compiler_params=pltpu.CompilerParams(
            collective_id=1 if packed else 0, has_side_effects=True, vmem_limit_bytes=58 << 20
        ),
    )(band_start, band_count, fir_taps, stations, voltages)


def place_kernel(in_ref, mask_ref, out_ref, scratch):
    mask = mask_ref[...]
    for q in range(CMAX):
        for o in range(2):
            values = in_ref[q, o].astype(f32) * mask
            for part in range(8):
                for half in range(2):
                    scratch[part, pl.ds(half * 256 + o * 16 + q, 8, stride=32), :] = values[
                        half * 8 : (half + 1) * 8, part * 128 : (part + 1) * 128
                    ]
    for part in range(8):
        out_ref[:, part * 128 : (part + 1) * 128] = scratch[part]


def place(blocks, mask):
    slots, _, rows, inputs = blocks.shape
    flat = pl.pallas_call(
        place_kernel,
        name="place",
        grid=(rows // 16,),
        out_shape=jax.ShapeDtypeStruct((rows * 2 * slots, inputs), f32),
        in_specs=[
            pl.BlockSpec((slots, 2, 16, inputs), lambda b: (0, 0, b, 0)),
            pl.BlockSpec((16, inputs), lambda b: (b, 0)),
        ],
        out_specs=pl.BlockSpec((16 * 2 * slots, inputs), lambda b: (b, 0)),
        scratch_shapes=[pltpu.VMEM((8, 16 * 2 * slots, 128), f32)],
        compiler_params=pltpu.CompilerParams(vmem_limit_bytes=60 << 20),
    )(blocks, mask)
    return flat.reshape(rows, 2, slots, inputs)


def unpack_kernel(subarray_ref, in_ref, place_ref, stations_ref, out_ref, scratch, spread):
    slots, rows, _ = in_ref.shape

    @pl.when(pl.program_id(0) == 0)
    def _():
        place = place_ref[...]
        row = lax.broadcasted_iota(jnp.int32, (MAIN, place.shape[1]), 0).astype(f32)
        main = jnp.where(row == place, f32(1), f32(0)).astype(bf16)
        rest = jnp.where(row[:REST] + MAIN == place, f32(1), f32(0)).astype(bf16)
        for o in range(2):
            spread[o, 0:MAIN] = main
            spread[o, MAIN + o * REST : ROOM + o * REST] = rest
            spread[o, ROOM - o * REST : WIDE - o * REST] = jnp.zeros_like(rest)

    for q in range(slots):
        values = in_ref[q].astype(f32)
        for part in range(2 * ROOM // 128):
            for half in range(rows // 8):
                scratch[part, pl.ds(half * 8 * slots + q, 8, stride=slots), :] = values[
                    half * 8 : (half + 1) * 8, part * 128 : (part + 1) * 128
                ]
    stations = stations_ref[...]
    masks = []
    first = (lax.axis_index("stn") * pl.num_programs(0) + pl.program_id(0)) * (rows // 2)
    for i in range(rows // 2):
        kind = subarray_ref[first + i].astype(f32)
        masks.append(jnp.where(stations == kind, f32(1.0 / SPECTRA), f32(0)))
    for o in range(2):
        packed = [scratch[part].astype(bf16) for part in (2 * o, 2 * o + 1, 4)]
        total = jnp.dot(jnp.concatenate(packed, axis=1), spread[o], preferred_element_type=f32)
        for i in range(rows):
            out_ref[i, o] = total[i * slots : (i + 1) * slots, :] * masks[i // 2]


def unpack(blocks, placing, stations, subarray):
    slots, rows, _ = blocks.shape
    inputs = stations.shape[1]
    return pl.pallas_call(
        unpack_kernel,
        name="unpack",
        grid=(rows // 16,),
        out_shape=jax.ShapeDtypeStruct((rows, 2, slots, inputs), f32),
        in_specs=[
            pl.BlockSpec(memory_space=pltpu.SMEM),
            pl.BlockSpec((slots, 16, 2 * ROOM), lambda b: (0, b, 0)),
            pl.BlockSpec((1, inputs), lambda b: (0, 0)),
            pl.BlockSpec((1, inputs), lambda b: (0, 0)),
        ],
        out_specs=pl.BlockSpec((16, 2, slots, inputs), lambda b: (b, 0, 0, 0)),
        scratch_shapes=[
            pltpu.VMEM((2 * ROOM // 128, 16 * slots, 128), f32),
            pltpu.VMEM((2, WIDE, inputs), bf16),
        ],
        compiler_params=pltpu.CompilerParams(vmem_limit_bytes=60 << 20),
    )(subarray, blocks, placing, stations)


def prepare_kernel(subarray_ref, stations_ref, fits_ref):
    kinds = jnp.broadcast_to(subarray_ref[...], (16, subarray_ref.shape[1])).astype(f32)
    row = lax.broadcasted_iota(jnp.int32, (16, subarray_ref.shape[1]), 0).astype(f32)
    sizes = jnp.sum(jnp.where(kinds == row, f32(1), f32(0)), axis=1, keepdims=True)
    fits_ref[0] = jnp.where(jnp.max(sizes) * 2 <= ROOM, 1, 0)
    shape = (subarray_ref.shape[1], stations_ref.shape[1])
    station = lax.broadcasted_iota(jnp.int32, shape, 0) * 2
    column = lax.broadcasted_iota(jnp.int32, shape, 1)
    twice = jnp.where((column - station == 0) | (column - station == 1), f32(1), f32(0))
    stations = jnp.dot(kinds.astype(bf16), twice.astype(bf16), preferred_element_type=f32)
    stations_ref[...] = stations[0:1]


def prepare(subarray):
    return pl.pallas_call(
        prepare_kernel,
        name="prepare",
        out_shape=(
            jax.ShapeDtypeStruct((1, 2 * subarray.shape[0]), f32),
            jax.ShapeDtypeStruct((1,), jnp.int32),
        ),
        in_specs=[pl.BlockSpec(memory_space=pltpu.VMEM)],
        out_specs=(pl.BlockSpec(memory_space=pltpu.VMEM), pl.BlockSpec(memory_space=pltpu.SMEM)),
    )(subarray[None, :])


def per_device(voltages, fir_taps, band_start, band_count, subarray):
    stations, fits = prepare(subarray)

    def packed_way():
        blocks, placing = correlator(True, voltages, fir_taps, band_start, band_count, stations)
        return unpack(blocks, placing, stations, subarray)

    def full_way():
        blocks, _ = correlator(False, voltages, fir_taps, band_start, band_count, stations)
        rows = blocks.shape[2]
        own = lax.dynamic_slice_in_dim(stations, lax.axis_index("stn") * rows, rows, 1)
        return place(blocks, (own.T == stations).astype(f32) / SPECTRA)

    return lax.cond(fits[0] == 1, packed_way, full_way)


def solution(mesh):
    in_specs = (P(None, ("stn", "chan"), None), P(), P(), P(), P())
    out_specs = P("stn", None, "chan", None)
    return jax.shard_map(
        per_device, mesh=mesh, in_specs=in_specs, out_specs=out_specs, check_vma=False
    )
```
